512 devices in a mesh: pulse: 128 (over x_hi, z, y), range: 4 (over x_lo, core).
Axes of the slice: x: 4 (x_hi: 2, x_lo: 2; x = x_hi * 2 + x_lo), y: 8, z: 8, core: 2. Of those that a mesh axis runs over, the one named last changes fastest.
Arguments:
- grad_image: bfloat16 [128, 2, 16, 16, 2048], P('pulse', None, None, None, 'range'), may hold values from -6 to 6
- range_kernel: bfloat16 [4, 16, 2, 128, 256], P(None, 'range'), may hold values from -0.25 to 0.25
- band_offsets: int32 [4, 16], P(None, 'range'), may hold values from -64 to 64
- beam_mix: bfloat16 [4, 128, 2, 8, 16], P(None, 'pulse'), may hold values from -1.5 to 1.5
- ramp: bfloat16 [4, 128, 2, 8, 2048], P(None, 'pulse', None, None, 'range'), may hold values from -3.140625 to 3.140625
- baseline_ids: int32 [16], replicated, may hold values from 0 to 7
- baseline_scale: float32 [8], replicated, may hold values from 0.5 to 2
Outputs:
- split_grad: bfloat16 [128, 2, 16, 16, 2048], P('pulse', None, None, None, 'range')
The draws below stay inside these ranges and needn't reach their ends.
All inputs are finite; a program needn't handle non-finite values.
Results may differ from the reference program's by a relative error of at most 0.017.
Values may be sent and summed in bfloat16 or wider, within the bound.
No kernel may reach another device: no remote copies, remote signals or barrier semaphores. Data moves between devices by JAX's collectives and lax.ppermute only.
A program may use at most 128 MiB of HBM per device.

```python
import math
import jax
import jax.numpy as jnp
from jax import lax

CH = 16
M_DEV = 16
TILE = 128
LEVELS = 4
NBASE = 8
P_SIZE = 128
R = 2048
NRT = 16


def place_ends(drawn, stream_key, low, top_value):
    place = [jax.random.randint(jax.random.fold_in(stream_key, axis), (), 0, length) for axis, length in enumerate(drawn.shape)]
    longest = drawn.shape.index(max(drawn.shape))
    beside = place[:longest] + [(place[longest] + 1) % drawn.shape[longest]] + place[longest + 1:]
    return drawn.at[tuple(place)].set(low).at[tuple(beside)].set(top_value)


def block_scale(own_key, shape, cuts, smallest, high):
    def one(axis_at, parts):
        heights = jax.random.uniform(jax.random.fold_in(jax.random.fold_in(own_key, 6), axis_at), (parts,), jnp.float32, smallest / len(cuts), high / len(cuts))
        return jnp.repeat(jnp.exp(heights), shape[axis_at] // parts).reshape((-1,) + (1,) * (len(shape) - axis_at - 1))

    gain = one(*cuts[0])
    for cut in cuts[1:]:
        gain = gain * one(*cut)
    return gain


def scatter_about(stream_key, dims, deviation, limit, cuts=(), kind=jnp.bfloat16):
    loudness = block_scale(stream_key, dims, cuts, -0.22, 0.18) if cuts else 1.0
    result = jax.random.normal(stream_key, dims, jnp.float32) * deviation * loudness
    return jnp.minimum(jnp.maximum(result, -limit), limit).astype(kind)


def setup_inputs(seed: int = 0) -> dict:
    arg_keys = jax.random.split(jax.random.key(seed), 8)
    return {
        "grad_image": scatter_about(arg_keys[0], (P_SIZE, 2, CH, M_DEV, R), 1.0, 6.0, ((0, 128), (4, 4))),
        "range_kernel": scatter_about(arg_keys[1], (LEVELS, NRT, 2, TILE, 2 * TILE), (4 * TILE) ** -0.5, 0.25, ((1, 4),)),
        "band_offsets": place_ends(jax.random.randint(arg_keys[2], (LEVELS, NRT), 0 - TILE // 2, TILE // 2 + 1), jax.random.fold_in(arg_keys[2], 1), 0 - TILE // 2, (TILE // 2 + 1) - 1).astype(jnp.int32),
        "beam_mix": scatter_about(arg_keys[3], (LEVELS, P_SIZE, 2, M_DEV // 2, M_DEV), M_DEV ** -0.5, 1.5, ((1, 128),)),
        "ramp": jnp.clip(jax.random.uniform(arg_keys[4], (LEVELS, P_SIZE, 2, M_DEV // 2, R), jnp.float32, -3.140625, 3.140625), -3.140625, 3.140625).astype(jnp.bfloat16),
        "baseline_ids": place_ends(jax.random.randint(arg_keys[5], (CH,), 0, NBASE), jax.random.fold_in(arg_keys[5], 1), 0, NBASE - 1).astype(jnp.int32),
        "baseline_scale": jnp.clip(jnp.exp(jax.random.uniform(arg_keys[6], (NBASE,), jnp.float32, math.log(0.5), math.log(2.0))), 0.5, 2.0),
    }


def slot_level(slot_grad, kernel, offsets, mixing, ramp_slot, channel_phase):
    padded = jnp.pad(slot_grad, ((0, 0), (0, 0), (0, 0), (TILE, TILE)))
    tile_count = kernel.shape[0]
    starts = (jnp.arange(tile_count, dtype=jnp.int32) * TILE + TILE // 2 + offsets.astype(jnp.int32)).astype(jnp.int32)
    windows = jax.vmap(lambda begin: lax.dynamic_slice_in_dim(padded, begin, 2 * TILE, 3))(starts)
    windows = windows.astype(jnp.float32)
    kernel = kernel.astype(jnp.float32)
    real_in, imag_in = windows[:, 0], windows[:, 1]
    kern_re, kern_im = kernel[:, 0], kernel[:, 1]
    real_out = jnp.einsum("tcmk,tok->cmto", real_in, kern_re) - jnp.einsum("tcmk,tok->cmto", imag_in, kern_im)
    imag_out = jnp.einsum("tcmk,tok->cmto", real_in, kern_im) + jnp.einsum("tcmk,tok->cmto", imag_in, kern_re)
    inner_shape = slot_grad.shape[1:]
    interp = jnp.stack([real_out.reshape(inner_shape), imag_out.reshape(inner_shape)]).astype(jnp.bfloat16)
    mixed = jnp.einsum("zcmr,dnm->dzcnr", interp.astype(jnp.float32), mixing.astype(jnp.float32))
    theta = ramp_slot.astype(jnp.float32)[:, None, :, :] * channel_phase[None, :, None, None]
    cosine = jnp.cos(theta)
    sine = jnp.sin(theta)
    mixed_re = mixed[:, 0]
    mixed_im = mixed[:, 1]
    out_re = mixed_re * cosine + mixed_im * sine
    out_im = mixed_im * cosine - mixed_re * sine
    return jnp.stack([out_re, out_im], axis=1).astype(jnp.bfloat16)


def reference(grad_image, range_kernel, band_offsets, beam_mix, ramp, baseline_ids, baseline_scale):
    channel_phase = baseline_scale[baseline_ids]
    current = grad_image
    slots = current.shape[0]
    log_slots = slots.bit_length() - 1
    for level_index in range(LEVELS):
        bit_number = (log_slots - 3 - level_index) % log_slots
        kernel = range_kernel[level_index]
        offsets = band_offsets[level_index]

        def per_slot(items):
            return slot_level(items[0], kernel, offsets, items[1], items[2], channel_phase)

        halves = lax.map(per_slot, (current, beam_mix[level_index], ramp[level_index]))
        span = 2 ** bit_number
        blocks = halves.reshape((slots // (2 * span), 2, span) + halves.shape[1:])
        moved = jnp.transpose(blocks, (0, 3, 2, 4, 5, 1, 6, 7))
        current = moved.reshape(current.shape)
    return current
```

```python
import functools
import jax
import jax.numpy as jnp
from jax import lax
from jax.experimental import pallas as pl
from jax.experimental.pallas import tpu as pltpu
from jax.sharding import PartitionSpec as P

TILE = 128
LEVELS = 4
CHANNELS = 16
BEAMS = 8
PART = CHANNELS * BEAMS
BITS = (4, 3, 2, 1)
BLOCK = 512
TILES = BLOCK // TILE
VMEM_LIMIT = 24 * 1024 * 1024
BF = jnp.bfloat16
F32 = jnp.float32
VMEM = pl.BlockSpec(memory_space=pltpu.VMEM)


def call(kernel, out_shape, count, flops, name, scratch=()):
    return pl.pallas_call(
        kernel,
        out_shape=out_shape,
        in_specs=[VMEM] * count,
        out_specs=[VMEM] * len(out_shape),
        scratch_shapes=list(scratch),
        compiler_params=pltpu.CompilerParams(vmem_limit_bytes=VMEM_LIMIT),
        cost_estimate=pl.CostEstimate(flops=flops, bytes_accessed=1 << 20, transcendentals=0),
        name=name,
    )


def shape(*dims, dtype=BF):
    return jax.ShapeDtypeStruct(dims, dtype)


def is_odd():
    return lax.axis_index("range") % 2 == 1


def bit_of(level):
    return lax.axis_index("pulse") // 2 ** BITS[level] % 2


def aligned(lane):
    return pl.multiple_of(lane, TILE)


def sincos(theta):
    turns = jnp.round(theta * 0.6366197723675814)
    rest = theta - turns * 1.5703125
    rest = rest - turns * 4.837512969970703e-4
    rest = rest - turns * 7.549789948768648e-8
    sq = rest * rest
    sine = rest + rest * sq * (-1.6666654611e-1 + sq * (8.3321608736e-3 - sq * 1.9515295891e-4))
    cosine = 1.0 - 0.5 * sq + sq * sq * (
        4.166664568298827e-2 + sq * (-1.388731625493765e-3 + sq * 2.443315711809948e-5)
    )
    quarter = turns.astype(jnp.int32)
    odd = (quarter & 1) == 1
    sin_sign = (quarter & 2) == 2
    cos_sign = ((quarter + 1) & 2) == 2
    out_sin = jnp.where(odd, cosine, sine)
    out_cos = jnp.where(odd, sine, cosine)
    return jnp.where(sin_sign, -out_sin, out_sin), jnp.where(cos_sign, -out_cos, out_cos)


def tables_kernel(level, taps, offsets, ramp, ids, scale, beam, shifted, cos_ref, sin_ref, mix_ref):
    row = lax.broadcasted_iota(jnp.int32, (2 * TILE, 3 * TILE), 0)
    col = lax.broadcasted_iota(jnp.int32, (2 * TILE, 3 * TILE), 1)
    gap = (col - row).astype(F32) - TILE // 2
    moves = offsets[...].astype(F32)
    for tile in range(TILES):
        pick = jnp.where(gap == moves[level : level + 1, tile : tile + 1], 1.0, 0.0).astype(BF)
        flat = taps[0, tile].reshape(2 * TILE, 2 * TILE)
        shifted[tile] = jnp.dot(flat, pick, preferred_element_type=F32).astype(BF)

    phase = jnp.zeros((1, CHANNELS), F32)
    for baseline in range(8):
        phase = phase + jnp.where(ids[...] == baseline, scale[:, baseline : baseline + 1], 0.0)
    bit = bit_of(level)
    angles = ramp[0, 0].astype(F32)
    sent = jnp.where(bit == 1, angles[0], angles[1])
    held = jnp.where(bit == 1, angles[1], angles[0])
    for channel in range(CHANNELS):
        length = phase[:, channel : channel + 1]
        for side, angle in enumerate((sent, held)):
            sine, cosine = sincos(angle * length)
            at = pl.ds(side * PART + channel * BEAMS, BEAMS)
            cos_ref[at, :] = cosine
            sin_ref[at, :] = sine

    size = 2 * PART
    row = lax.broadcasted_iota(jnp.int32, (size, 16), 0)
    want = lax.broadcasted_iota(jnp.int32, (size, 16), 1)
    child = jnp.where(row // PART == 1, bit, 1 - bit)
    choose = jnp.where(want == child * BEAMS + row % BEAMS, 1.0, 0.0).astype(BF)
    beams = beam[0, 0].astype(F32).reshape(16, 16).astype(BF)
    rows = jnp.dot(choose, beams, preferred_element_type=F32).astype(BF)
    have = lax.broadcasted_iota(jnp.int32, (16, size), 0)
    col = lax.broadcasted_iota(jnp.int32, (16, size), 1)
    if level == 0:
        source = col % 16
    else:
        before = bit_of(level - 1)
        source = jnp.where(col // PART == 0, before, 1 - before) * BEAMS + col % BEAMS
    spread = jnp.where(have == source, 1.0, 0.0).astype(BF)
    full = jnp.dot(rows, spread, preferred_element_type=F32)
    at_row = lax.broadcasted_iota(jnp.int32, (size, size), 0) // BEAMS % CHANNELS
    at_col = lax.broadcasted_iota(jnp.int32, (size, size), 1)
    at_col = at_col // 16 if level == 0 else at_col // BEAMS % CHANNELS
    mix_ref[...] = jnp.where(at_row == at_col, full, 0.0).astype(BF)


def make_tables(level, taps, offsets, ramp, ids, scale, beam_mix):
    part = pl.BlockSpec((1, TILES, 2, TILE, 2 * TILE), lambda i: (level, 0, 0, 0, 0))
    angle = pl.BlockSpec((1, 1, 2, BEAMS, BLOCK), lambda i: (level, 0, 0, 0, 0))
    beam = pl.BlockSpec((1, 1, 2, BEAMS, 16), lambda i: (level, 0, 0, 0, 0))
    angles = shape(2 * PART, BLOCK, dtype=F32)
    return pl.pallas_call(
        functools.partial(tables_kernel, level),
        grid=(1,),
        out_shape=[shape(TILES, 2 * TILE, 3 * TILE), angles, angles, shape(2 * PART, 2 * PART)],
        in_specs=[part, VMEM, angle, VMEM, VMEM, beam],
        out_specs=[VMEM] * 4,
        compiler_params=pltpu.CompilerParams(vmem_limit_bytes=VMEM_LIMIT),
        cost_estimate=pl.CostEstimate(flops=1 << 27, bytes_accessed=1 << 21, transcendentals=0),
        name=f"tables{level}",
    )(taps, offsets, ramp, ids, scale, beam_mix)


def merge(spread, shifted, cos_ref, sin_ref, mix_ref, write):
    rows = 2 * PART
    mix = mix_ref[...]
    parts = []
    for tile in range(TILES):
        window = spread[:, tile * TILE : (tile + 3) * TILE]
        both = lax.dot_general(window, shifted[tile], (((1,), (1,)), ((), ())), preferred_element_type=F32)
        real = both[:rows, :TILE] - both[rows:, TILE:]
        imag = both[:rows, TILE:] + both[rows:, :TILE]
        parts.append(jnp.concatenate([real, imag], axis=1).astype(BF))
    for tile in range(TILES):
        lanes = slice(tile * TILE, (tile + 1) * TILE)
        mixed = jnp.dot(mix, parts[tile], preferred_element_type=F32)
        mixed_re = mixed[:, :TILE]
        mixed_im = mixed[:, TILE:]
        cosine = cos_ref[:, lanes]
        sine = sin_ref[:, lanes]
        out_re = (mixed_re * cosine + mixed_im * sine).astype(BF)
        out_im = (mixed_im * cosine - mixed_re * sine).astype(BF)
        write(lanes, out_re, out_im)


def level_kernel(level, *refs):
    count = 3 if level == 0 else 6
    data, rest = refs[:count], refs[count:]
    tables, rest = rest[:4], rest[4:]
    *outs, spread = rest
    odd = is_odd()
    near = pl.ds(aligned(jnp.where(odd, 0, BLOCK + TILE)), TILE)
    far = pl.ds(aligned(jnp.where(odd, BLOCK + TILE, 0)), TILE)
    middle = pl.ds(TILE, BLOCK)
    if level == 0:
        block, near_edge, far_edge = data
        for z in range(2):
            rows = pl.ds(2 * z * PART, 2 * PART)
            spread[rows, middle] = block[z].reshape(2 * PART, BLOCK)
            spread[rows, near] = near_edge[z].reshape(2 * PART, TILE)
            spread[rows, far] = far_edge[z].reshape(2 * PART, TILE)
    else:
        for side in range(2):
            block, near_edge, far_edge = data[3 * side : 3 * side + 3]
            for z in range(2):
                rows = pl.ds((2 * z + side) * PART, PART)
                spread[rows, middle] = block[z]
                spread[rows, near] = near_edge[z]
                spread[rows, far] = far_edge[z]
    edges = level < LEVELS - 1
    held, sent = outs[0], outs[3 if edges else 1]

    def write(lanes, out_re, out_im):
        for z, value in enumerate((out_re, out_im)):
            sent[z, :, lanes] = value[:PART]
            held[z, :, lanes] = value[PART:]

    merge(spread, *tables, write)
    if edges:
        high = pl.ds(aligned(jnp.where(odd, 0, BLOCK - TILE)), TILE)
        low = pl.ds(aligned(jnp.where(odd, BLOCK - TILE, 0)), TILE)
        for block, near_edge, far_edge in (outs[:3], outs[3:]):
            near_edge[...] = block[:, :, high]
            far_edge[...] = block[:, :, low]


def level_call(level, data, tables):
    edge = shape(2, PART, TILE)
    block = shape(2, PART, BLOCK)
    outs = [block] * 2 if level == LEVELS - 1 else [block, edge, edge] * 2
    operands = (*data, *tables)
    return call(
        functools.partial(level_kernel, level),
        outs,
        len(operands),
        TILES * 2 * (4 * PART * 384 * 256 + 4 * PART * PART * 256),
        f"merge{level}",
        [pltpu.VMEM((4 * PART, BLOCK + 2 * TILE), BF)],
    )(*operands)


def body(grad_image, range_kernel, band_offsets, beam_mix, ramp, baseline_ids, baseline_scale):
    pulses = lax.axis_size("pulse")
    ranges = lax.axis_size("range")
    near_pairs = [(i, i ^ 1) for i in range(ranges)]
    far_pairs = [(i, i + 1) for i in range(1, ranges - 1, 2)]
    far_pairs += [(t, s) for s, t in far_pairs]

    def move(value, mask, pairs):
        pairs = [(p * ranges + s, (p ^ mask) * ranges + t) for p in range(pulses) for s, t in pairs]
        return lax.ppermute(value, ("pulse", "range"), pairs)

    block = grad_image[0]
    low = block[..., :TILE]
    high = block[..., BLOCK - TILE :]
    odd = is_odd()
    far_edge = move(jnp.where(odd, high, low), 0, far_pairs)
    near_edge = move(jnp.where(odd, low, high), 0, near_pairs)
    state = (block, near_edge, far_edge)
    for level in range(LEVELS):
        tables = make_tables(
            level, range_kernel, band_offsets, ramp, baseline_ids[None], baseline_scale[None], beam_mix
        )
        outs = level_call(level, state, tables)
        mask = 2 ** BITS[level]
        stay = [(i, i) for i in range(ranges)]
        if level < LEVELS - 1:
            held, held_near, held_far, sent, sent_near, sent_far = outs
            got = move(sent, mask, stay)
            state = (
                held,
                move(held_near, 0, near_pairs),
                move(held_far, 0, far_pairs),
                got,
                move(sent_near, mask, near_pairs),
                move(sent_far, mask, far_pairs),
            )
        else:
            held, sent = outs
            got = move(sent, mask, stay)

    held = held.reshape(2, CHANNELS, BEAMS, BLOCK)
    got = got.reshape(2, CHANNELS, BEAMS, BLOCK)
    mine = bit_of(LEVELS - 1) == 1
    return jnp.concatenate([jnp.where(mine, got, held), jnp.where(mine, held, got)], axis=2)[None]


def solution(mesh):
    placed = (
        P("pulse", None, None, None, "range"),
        P(None, "range", None, None, None),
        P(None, "range"),
        P(None, "pulse", None, None, None),
        P(None, "pulse", None, None, "range"),
        P(),
        P(),
    )
    return jax.shard_map(
        body,
        mesh=mesh,
        in_specs=placed,
        out_specs=P("pulse", None, None, None, "range"),
        check_vma=False,
    )
```

```python
import functools
import jax
import jax.numpy as jnp
from jax import lax
from jax.experimental import pallas as pl
from jax.experimental.pallas import tpu as pltpu
from jax.sharding import PartitionSpec as P

TILE = 128
LEVELS = 4
CHANNELS = 16
BEAMS = 8
PART = CHANNELS * BEAMS
BITS = (4, 3, 2, 1)
BLOCK = 512
TILES = BLOCK // TILE
VMEM_LIMIT = 24 * 1024 * 1024
BF = jnp.bfloat16
F32 = jnp.float32
VMEM = pl.BlockSpec(memory_space=pltpu.VMEM)
ANYWHERE = pl.BlockSpec(memory_space=pl.ANY)
WIDE = (0, 2)
REACH = 2 * TILE
KERNEL_AT = 32
RAMP_AT = KERNEL_AT + 16 * len(WIDE)
UNITS = RAMP_AT + len(WIDE)


def call(kernel, out_shape, count, flops, name, scratch=()):
    return pl.pallas_call(
        kernel,
        out_shape=out_shape,
        in_specs=[VMEM] * count,
        out_specs=[VMEM] * len(out_shape),
        scratch_shapes=list(scratch),
        compiler_params=pltpu.CompilerParams(vmem_limit_bytes=VMEM_LIMIT),
        cost_estimate=pl.CostEstimate(flops=flops, bytes_accessed=1 << 20, transcendentals=0),
        name=name,
    )


def shape(*dims, dtype=BF):
    return jax.ShapeDtypeStruct(dims, dtype)


def is_odd():
    return lax.axis_index("range") % 2 == 1


def bit_of(level):
    return lax.axis_index("pulse") // 2 ** BITS[level] % 2


def aligned(lane):
    return pl.multiple_of(lane, TILE)


def sincos(theta):
    turns = jnp.round(theta * 0.6366197723675814)
    rest = theta - turns * 1.5703125
    rest = rest - turns * 4.837512969970703e-4
    rest = rest - turns * 7.549789948768648e-8
    sq = rest * rest
    sine = rest + rest * sq * (-1.6666654611e-1 + sq * (8.3321608736e-3 - sq * 1.9515295891e-4))
    cosine = 1.0 - 0.5 * sq + sq * sq * (
        4.166664568298827e-2 + sq * (-1.388731625493765e-3 + sq * 2.443315711809948e-5)
    )
    quarter = turns.astype(jnp.int32)
    odd = (quarter & 1) == 1
    sin_sign = (quarter & 2) == 2
    cos_sign = ((quarter + 1) & 2) == 2
    out_sin = jnp.where(odd, cosine, sine)
    out_cos = jnp.where(odd, sine, cosine)
    return jnp.where(sin_sign, -out_sin, out_sin), jnp.where(cos_sign, -out_cos, out_cos)


def edges_kernel(image, taps, ramp, offsets, near, far, moves, sems):
    odd = is_odd()
    near_lanes = pl.ds(aligned(jnp.where(odd, 0, BLOCK - REACH)), REACH)
    far_lanes = pl.ds(aligned(jnp.where(odd, BLOCK - TILE, 0)), TILE)
    ramp_lanes = pl.ds(aligned(jnp.where(odd, 0, BLOCK - TILE)), TILE)
    copies = [(offsets, moves)]
    for z in range(2):
        copies.append((image.at[z, :, :, near_lanes], near.at[pl.ds(16 * z, 16)]))
        copies.append((image.at[z, :, :, far_lanes], far.at[z]))
    for at, level in enumerate(WIDE):
        copies.append((taps.at[level, jnp.where(odd, 0, TILES - 1)], near.at[pl.ds(KERNEL_AT + 16 * at, 16)]))
        copies.append((ramp.at[level, :, ramp_lanes], near.at[RAMP_AT + at, :, pl.ds(0, TILE)]))
    copies = [pltpu.make_async_copy(s, t, sems.at[i]) for i, (s, t) in enumerate(copies)]
    for copy in copies:
        copy.start()
    copies[0].wait()
    values = moves[...].astype(F32)
    for at, level in enumerate(WIDE):
        row = values[level : level + 1]
        value = jnp.where(odd, row[:, 0:1], row[:, TILES - 1 : TILES])
        near[RAMP_AT + at, :, TILE:] = jnp.broadcast_to(value, (16, REACH - TILE)).astype(BF)
    for copy in copies[1:]:
        copy.wait()


def take_edges(image, taps, ramp, offsets):
    return pl.pallas_call(
        edges_kernel,
        out_shape=[shape(UNITS, 16, REACH), shape(2, CHANNELS, 2 * BEAMS, TILE)],
        in_specs=[ANYWHERE] * 4,
        out_specs=[VMEM] * 2,
        scratch_shapes=[pltpu.VMEM((LEVELS, TILES), jnp.int32), pltpu.SemaphoreType.DMA((9,))],
        compiler_params=pltpu.CompilerParams(vmem_limit_bytes=56 * 1024 * 1024),
        cost_estimate=pl.CostEstimate(flops=1 << 20, bytes_accessed=1 << 20, transcendentals=0),
        name="edges",
    )(image, taps, ramp, offsets)


def put_shifted(shifted, tile, taps, offset):
    row = lax.broadcasted_iota(jnp.int32, (2 * TILE, 3 * TILE), 0)
    col = lax.broadcasted_iota(jnp.int32, (2 * TILE, 3 * TILE), 1)
    gap = (col - row).astype(F32) - TILE // 2
    pick = jnp.where(gap == offset, 1.0, 0.0).astype(BF)
    flat = taps.reshape(2 * TILE, 2 * TILE)
    shifted[tile] = jnp.dot(flat, pick, preferred_element_type=F32).astype(BF)


def put_angles(level, cos_ref, sin_ref, ids, scale, first, second):
    phase = jnp.zeros((1, CHANNELS), F32)
    for baseline in range(8):
        phase = phase + jnp.where(ids[...] == baseline, scale[:, baseline : baseline + 1], 0.0)
    bit = bit_of(level)
    sent = jnp.where(bit == 1, first, second)
    held = jnp.where(bit == 1, second, first)
    for channel in range(CHANNELS):
        length = phase[:, channel : channel + 1]
        for side, angle in enumerate((sent, held)):
            sine, cosine = sincos(angle * length)
            at = pl.ds(side * PART + channel * BEAMS, BEAMS)
            cos_ref[at, :] = cosine
            sin_ref[at, :] = sine


def tables_kernel(level, taps, offsets, ramp, ids, scale, beam, shifted, cos_ref, sin_ref, mix_ref):
    moves = offsets[...].astype(F32)
    for tile in range(TILES):
        put_shifted(shifted, tile, taps[0, tile], moves[level : level + 1, tile : tile + 1])
    angles = ramp[0, 0].astype(F32)
    put_angles(level, cos_ref, sin_ref, ids, scale, angles[0], angles[1])

    size = 2 * PART
    bit = bit_of(level)
    row = lax.broadcasted_iota(jnp.int32, (size, 16), 0)
    want = lax.broadcasted_iota(jnp.int32, (size, 16), 1)
    child = jnp.where(row // PART == 1, bit, 1 - bit)
    choose = jnp.where(want == child * BEAMS + row % BEAMS, 1.0, 0.0).astype(BF)
    beams = beam[0, 0].astype(F32).reshape(16, 16).astype(BF)
    rows = jnp.dot(choose, beams, preferred_element_type=F32).astype(BF)
    have = lax.broadcasted_iota(jnp.int32, (16, size), 0)
    col = lax.broadcasted_iota(jnp.int32, (16, size), 1)
    if level == 0:
        source = col % 16
    else:
        before = bit_of(level - 1)
        source = jnp.where(col // PART == 0, before, 1 - before) * BEAMS + col % BEAMS
    spread = jnp.where(have == source, 1.0, 0.0).astype(BF)
    full = jnp.dot(rows, spread, preferred_element_type=F32)
    at_row = lax.broadcasted_iota(jnp.int32, (size, size), 0) // BEAMS % CHANNELS
    at_col = lax.broadcasted_iota(jnp.int32, (size, size), 1)
    at_col = at_col // 16 if level == 0 else at_col // BEAMS % CHANNELS
    mix_ref[...] = jnp.where(at_row == at_col, full, 0.0).astype(BF)


def make_tables(level, taps, offsets, ramp, ids, scale, beam_mix):
    part = pl.BlockSpec((1, TILES, 2, TILE, 2 * TILE), lambda i: (level, 0, 0, 0, 0))
    angle = pl.BlockSpec((1, 1, 2, BEAMS, BLOCK), lambda i: (level, 0, 0, 0, 0))
    beam = pl.BlockSpec((1, 1, 2, BEAMS, 16), lambda i: (level, 0, 0, 0, 0))
    angles = shape(2 * PART, BLOCK, dtype=F32)
    return pl.pallas_call(
        functools.partial(tables_kernel, level),
        grid=(1,),
        out_shape=[shape(TILES, 2 * TILE, 3 * TILE), angles, angles, shape(2 * PART, 2 * PART)],
        in_specs=[part, VMEM, angle, VMEM, VMEM, beam],
        out_specs=[VMEM] * 4,
        compiler_params=pltpu.CompilerParams(vmem_limit_bytes=VMEM_LIMIT),
        cost_estimate=pl.CostEstimate(flops=1 << 27, bytes_accessed=1 << 21, transcendentals=0),
        name=f"tables{level}",
    )(taps, offsets, ramp, ids, scale, beam_mix)


def reach_kernel(level, near, ids, scale, shifted, cos_ref, sin_ref):
    at = WIDE.index(level)
    last = near[RAMP_AT + at].astype(F32)
    put_shifted(shifted, 0, near[KERNEL_AT + 16 * at : KERNEL_AT + 16 * (at + 1)], last[0:1, TILE : TILE + 1])
    put_angles(level, cos_ref, sin_ref, ids, scale, last[:BEAMS, :TILE], last[BEAMS:, :TILE])


def reach_tables(level, near, ids, scale):
    angles = shape(2 * PART, TILE, dtype=F32)
    outs = [shape(1, 2 * TILE, 3 * TILE), angles, angles]
    return call(functools.partial(reach_kernel, level), outs, 3, 1 << 25, f"reach{level}")(near, ids, scale)


def merge(spread, main, reach, mix, write):
    rows = 2 * PART
    wide = len(reach) > 0
    odd = jnp.where(is_odd(), 1, 0)
    order = [(main, tile, tile + odd if wide else tile) for tile in range(TILES)]
    if wide:
        order.append((reach, 0, jnp.where(odd == 1, 0, TILES)))
    parts = []
    for (shifted, _, _), index, place in order:
        window = spread[:, pl.ds(aligned(place * TILE), 3 * TILE)]
        both = lax.dot_general(window, shifted[index], (((1,), (1,)), ((), ())), preferred_element_type=F32)
        real = both[:rows, :TILE] - both[rows:, TILE:]
        imag = both[:rows, TILE:] + both[rows:, :TILE]
        parts.append(jnp.concatenate([real, imag], axis=1).astype(BF))
    for ((_, cos_ref, sin_ref), index, place), part in zip(order, parts):
        lanes = slice(index * TILE, (index + 1) * TILE)
        mixed = jnp.dot(mix, part, preferred_element_type=F32)
        mixed_re = mixed[:, :TILE]
        mixed_im = mixed[:, TILE:]
        cosine = cos_ref[:, lanes]
        sine = sin_ref[:, lanes]
        out_re = (mixed_re * cosine + mixed_im * sine).astype(BF)
        out_im = (mixed_im * cosine - mixed_re * sine).astype(BF)
        write(pl.ds(aligned(place * TILE), TILE), out_re, out_im)


def level_kernel(level, *refs):
    wide = level in WIDE
    count = 3 if level == 0 else 6 if wide else 4
    data, rest = refs[:count], refs[count:]
    main, mix_ref, rest = rest[:3], rest[3], rest[4:]
    reach = ()
    if wide:
        reach, rest = rest[:3], rest[3:]
    *outs, spread = rest
    odd = is_odd()
    if wide:
        near = pl.ds(aligned(jnp.where(odd, 0, BLOCK + TILE)), REACH)
        far = pl.ds(aligned(jnp.where(odd, BLOCK + REACH, 0)), TILE)
        middle = pl.ds(aligned(jnp.where(odd, REACH, TILE)), BLOCK)
    else:
        far = pl.ds(aligned(jnp.where(odd, BLOCK + TILE, 0)), TILE)
        middle = pl.ds(aligned(jnp.where(odd, 0, TILE)), BLOCK + TILE)
    if level == 0:
        block, near_edge, far_edge = data
        for z in range(2):
            rows = pl.ds(2 * z * PART, 2 * PART)
            spread[rows, middle] = block[z].reshape(2 * PART, BLOCK)
            spread[rows, near] = near_edge[pl.ds(16 * z, 16)].reshape(2 * PART, REACH)
            spread[rows, far] = far_edge[z].reshape(2 * PART, TILE)
    else:
        for side in range(2):
            for z in range(2):
                rows = pl.ds((2 * z + side) * PART, PART)
                spread[rows, middle] = data[side][z]
                spread[rows, far] = data[2 + side][z]
                if wide:
                    spread[rows, near] = data[4 + side][z]
    held, sent = outs[:2]

    def write(lanes, out_re, out_im):
        for z, value in enumerate((out_re, out_im)):
            sent[z, :, lanes] = value[:PART]
            held[z, :, lanes] = value[PART:]

    merge(spread, main, reach, mix_ref[...], write)
    if level < LEVELS - 1:
        start = BLOCK if wide else BLOCK - TILE
        far = pl.ds(aligned(jnp.where(odd, start, 0)), TILE)
        near = pl.ds(aligned(jnp.where(odd, 0, BLOCK - REACH)), REACH)
        for side in range(2):
            outs[2 + side][...] = outs[side][:, :, far]
            if not wide:
                outs[4 + side][...] = outs[side][:, :, near]


def level_call(level, data, tables, reach):
    wide = level in WIDE
    outs = [shape(2, PART, BLOCK + TILE if wide else BLOCK)] * 2
    if level < LEVELS - 1:
        outs += [shape(2, PART, TILE)] * 2
        if not wide:
            outs += [shape(2, PART, REACH)] * 2
    operands = (*data, *tables, *reach)
    width = BLOCK + TILE + (REACH if wide else TILE)
    return call(
        functools.partial(level_kernel, level),
        outs,
        len(operands),
        TILES * 2 * (4 * PART * 384 * 256 + 4 * PART * PART * 256),
        f"merge{level}",
        [pltpu.VMEM((4 * PART, width), BF)],
    )(*operands)


def body(grad_image, range_kernel, band_offsets, beam_mix, ramp, baseline_ids, baseline_scale):
    pulses = lax.axis_size("pulse")
    ranges = lax.axis_size("range")
    near_pairs = [(i, i ^ 1) for i in range(ranges)]
    far_pairs = [(i, i + 1) for i in range(1, ranges - 1, 2)]
    far_pairs += [(t, s) for s, t in far_pairs]

    def move(value, mask, pairs):
        pairs = [(p * ranges + s, (p ^ mask) * ranges + t) for p in range(pulses) for s, t in pairs]
        return lax.ppermute(value, ("pulse", "range"), pairs)

    block = grad_image[0]
    ids = baseline_ids[None]
    scale = baseline_scale[None]
    near_pack, far_edge = take_edges(
        block,
        range_kernel.reshape(LEVELS, TILES, 16, 16, 2 * TILE),
        ramp.reshape(LEVELS, 2 * BEAMS, BLOCK),
        band_offsets,
    )
    near_pack = move(near_pack, 0, near_pairs)
    far_edge = move(far_edge, 0, far_pairs)
    state = (block, near_pack, far_edge)
    stay = [(i, i) for i in range(ranges)]
    tables = [make_tables(l, range_kernel, band_offsets, ramp, ids, scale, beam_mix) for l in range(LEVELS)]
    reach = [reach_tables(l, near_pack, ids, scale) if l in WIDE else () for l in range(LEVELS)]
    for level in range(LEVELS):
        if level == 1:
            state, tables, reach = lax.optimization_barrier((state, tables, reach))
        held, sent, *edges = level_call(level, state, tables[level], reach[level])
        mask = 2 ** BITS[level]
        got = move(sent, mask, stay)
        state = [held, got]
        if edges:
            state += [move(edges[0], 0, far_pairs), move(edges[1], mask, far_pairs)]
        if len(edges) > 2:
            state += [move(edges[2], 0, near_pairs), move(edges[3], mask, near_pairs)]

    held = held.reshape(2, CHANNELS, BEAMS, BLOCK)
    got = got.reshape(2, CHANNELS, BEAMS, BLOCK)
    mine = bit_of(LEVELS - 1) == 1
    return jnp.concatenate([jnp.where(mine, got, held), jnp.where(mine, held, got)], axis=2)[None]


def solution(mesh):
    placed = (
        P("pulse", None, None, None, "range"),
        P(None, "range", None, None, None),
        P(None, "range"),
        P(None, "pulse", None, None, None),
        P(None, "pulse", None, None, "range"),
        P(),
        P(),
    )
    return jax.shard_map(
        body,
        mesh=mesh,
        in_specs=placed,
        out_specs=P("pulse", None, None, None, "range"),
        check_vma=False,
    )
```

```python
import functools
import jax
import jax.numpy as jnp
from jax import lax
from jax.experimental import pallas as pl
from jax.experimental.pallas import tpu as pltpu
from jax.sharding import PartitionSpec as P

TILE = 128
LEVELS = 4
CHANNELS = 16
BEAMS = 8
PART = CHANNELS * BEAMS
BITS = (4, 3, 2, 1)
BLOCK = 512
TILES = BLOCK // TILE
VMEM_LIMIT = 24 * 1024 * 1024
BF = jnp.bfloat16
F32 = jnp.float32
VMEM = pl.BlockSpec(memory_space=pltpu.VMEM)
ANYWHERE = pl.BlockSpec(memory_space=pl.ANY)
WIDE = (0, 2)
REACH = 2 * TILE
KERNEL_AT = 32
RAMP_AT = KERNEL_AT + 16 * len(WIDE)
UNITS = RAMP_AT + len(WIDE)


def call(kernel, out_shape, count, flops, name, scratch=()):
    return pl.pallas_call(
        kernel,
        out_shape=out_shape,
        in_specs=[VMEM] * count,
        out_specs=[VMEM] * len(out_shape),
        scratch_shapes=list(scratch),
        compiler_params=pltpu.CompilerParams(vmem_limit_bytes=VMEM_LIMIT),
        cost_estimate=pl.CostEstimate(flops=flops, bytes_accessed=1 << 20, transcendentals=0),
        name=name,
    )


def shape(*dims, dtype=BF):
    return jax.ShapeDtypeStruct(dims, dtype)


def is_odd():
    return lax.axis_index("range") % 2 == 1


def bit_of(level):
    return lax.axis_index("pulse") // 2 ** BITS[level] % 2


def aligned(lane):
    return pl.multiple_of(lane, TILE)


def sincos(theta):
    turns = jnp.round(theta * 0.6366197723675814)
    rest = theta - turns * 1.5703125
    rest = rest - turns * 4.837512969970703e-4
    rest = rest - turns * 7.549789948768648e-8
    sq = rest * rest
    sine = rest + rest * sq * (-1.6666654611e-1 + sq * (8.3321608736e-3 - sq * 1.9515295891e-4))
    cosine = 1.0 - 0.5 * sq + sq * sq * (
        4.166664568298827e-2 + sq * (-1.388731625493765e-3 + sq * 2.443315711809948e-5)
    )
    quarter = turns.astype(jnp.int32)
    odd = (quarter & 1) == 1
    sin_sign = (quarter & 2) == 2
    cos_sign = ((quarter + 1) & 2) == 2
    out_sin = jnp.where(odd, cosine, sine)
    out_cos = jnp.where(odd, sine, cosine)
    return jnp.where(sin_sign, -out_sin, out_sin), jnp.where(cos_sign, -out_cos, out_cos)


def edges_kernel(image, taps, ramp, offsets, near, far, moves, sems):
    odd = is_odd()
    near_lanes = pl.ds(aligned(jnp.where(odd, 0, BLOCK - REACH)), REACH)
    far_lanes = pl.ds(aligned(jnp.where(odd, BLOCK - TILE, 0)), TILE)
    ramp_lanes = pl.ds(aligned(jnp.where(odd, 0, BLOCK - TILE)), TILE)
    copies = [(offsets, moves)]
    for z in range(2):
        copies.append((image.at[z, :, :, near_lanes], near.at[pl.ds(16 * z, 16)]))
        copies.append((image.at[z, :, :, far_lanes], far.at[z]))
    for at, level in enumerate(WIDE):
        copies.append((taps.at[level, jnp.where(odd, 0, TILES - 1)], near.at[pl.ds(KERNEL_AT + 16 * at, 16)]))
        copies.append((ramp.at[level, :, ramp_lanes], near.at[RAMP_AT + at, :, pl.ds(0, TILE)]))
    copies = [pltpu.make_async_copy(s, t, sems.at[i]) for i, (s, t) in enumerate(copies)]
    for copy in copies:
        copy.start()
    copies[0].wait()
    values = moves[...].astype(F32)
    for at, level in enumerate(WIDE):
        row = values[level : level + 1]
        value = jnp.where(odd, row[:, 0:1], row[:, TILES - 1 : TILES])
        near[RAMP_AT + at, :, TILE:] = jnp.broadcast_to(value, (16, REACH - TILE)).astype(BF)
    for copy in copies[1:]:
        copy.wait()


def take_edges(image, taps, ramp, offsets):
    return pl.pallas_call(
        edges_kernel,
        out_shape=[shape(UNITS, 16, REACH), shape(2, CHANNELS, 2 * BEAMS, TILE)],
        in_specs=[ANYWHERE] * 4,
        out_specs=[VMEM] * 2,
        scratch_shapes=[pltpu.VMEM((LEVELS, TILES), jnp.int32), pltpu.SemaphoreType.DMA((9,))],
        compiler_params=pltpu.CompilerParams(vmem_limit_bytes=56 * 1024 * 1024),
        cost_estimate=pl.CostEstimate(flops=1 << 20, bytes_accessed=1 << 20, transcendentals=0),
        name="edges",
    )(image, taps, ramp, offsets)


def put_shifted(shifted, tile, taps, offset):
    row = lax.broadcasted_iota(jnp.int32, (2 * TILE, 3 * TILE), 0)
    col = lax.broadcasted_iota(jnp.int32, (2 * TILE, 3 * TILE), 1)
    gap = (col - row).astype(F32) - TILE // 2
    pick = jnp.where(gap == offset, 1.0, 0.0).astype(BF)
    flat = taps.reshape(2 * TILE, 2 * TILE)
    shifted[tile] = jnp.dot(flat, pick, preferred_element_type=F32).astype(BF)


def put_angles(level, cos_ref, sin_ref, ids, scale, first, second):
    phase = jnp.zeros((1, CHANNELS), F32)
    for baseline in range(8):
        phase = phase + jnp.where(ids[...] == baseline, scale[:, baseline : baseline + 1], 0.0)
    bit = bit_of(level)
    sent = jnp.where(bit == 1, first, second)
    held = jnp.where(bit == 1, second, first)
    for channel in range(CHANNELS):
        length = phase[:, channel : channel + 1]
        for side, angle in enumerate((sent, held)):
            sine, cosine = sincos(angle * length)
            at = pl.ds(side * PART + channel * BEAMS, BEAMS)
            cos_ref[at, :] = cosine
            sin_ref[at, :] = sine


def tables_kernel(level, taps, offsets, ramp, ids, scale, beam, shifted, cos_ref, sin_ref, mix_ref):
    moves = offsets[...].astype(F32)
    for tile in range(TILES):
        put_shifted(shifted, tile, taps[0, tile], moves[level : level + 1, tile : tile + 1])
    angles = ramp[0, 0].astype(F32)
    put_angles(level, cos_ref, sin_ref, ids, scale, angles[0], angles[1])

    size = 2 * PART
    bit = bit_of(level)
    row = lax.broadcasted_iota(jnp.int32, (size, 16), 0)
    want = lax.broadcasted_iota(jnp.int32, (size, 16), 1)
    child = jnp.where(row // PART == 1, bit, 1 - bit)
    choose = jnp.where(want == child * BEAMS + row % BEAMS, 1.0, 0.0).astype(BF)
    beams = beam[0, 0].astype(F32).reshape(16, 16).astype(BF)
    rows = jnp.dot(choose, beams, preferred_element_type=F32).astype(BF)
    have = lax.broadcasted_iota(jnp.int32, (16, size), 0)
    col = lax.broadcasted_iota(jnp.int32, (16, size), 1)
    if level == 0:
        source = col % 16
    else:
        before = bit_of(level - 1)
        source = jnp.where(col // PART == 0, before, 1 - before) * BEAMS + col % BEAMS
    spread = jnp.where(have == source, 1.0, 0.0).astype(BF)
    full = jnp.dot(rows, spread, preferred_element_type=F32)
    at_row = lax.broadcasted_iota(jnp.int32, (size, size), 0) // BEAMS % CHANNELS
    at_col = lax.broadcasted_iota(jnp.int32, (size, size), 1)
    at_col = at_col // 16 if level == 0 else at_col // BEAMS % CHANNELS
    mix_ref[...] = jnp.where(at_row == at_col, full, 0.0).astype(BF)


def make_tables(level, taps, offsets, ramp, ids, scale, beam_mix):
    part = pl.BlockSpec((1, TILES, 2, TILE, 2 * TILE), lambda i: (level, 0, 0, 0, 0))
    angle = pl.BlockSpec((1, 1, 2, BEAMS, BLOCK), lambda i: (level, 0, 0, 0, 0))
    beam = pl.BlockSpec((1, 1, 2, BEAMS, 16), lambda i: (level, 0, 0, 0, 0))
    angles = shape(2 * PART, BLOCK, dtype=F32)
    return pl.pallas_call(
        functools.partial(tables_kernel, level),
        grid=(1,),
        out_shape=[shape(TILES, 2 * TILE, 3 * TILE), angles, angles, shape(2 * PART, 2 * PART)],
        in_specs=[part, VMEM, angle, VMEM, VMEM, beam],
        out_specs=[VMEM] * 4,
        compiler_params=pltpu.CompilerParams(vmem_limit_bytes=VMEM_LIMIT),
        cost_estimate=pl.CostEstimate(flops=1 << 27, bytes_accessed=1 << 21, transcendentals=0),
        name=f"tables{level}",
    )(taps, offsets, ramp, ids, scale, beam_mix)


def reach_kernel(level, near, ids, scale, shifted, cos_ref, sin_ref):
    at = WIDE.index(level)
    last = near[RAMP_AT + at].astype(F32)
    put_shifted(shifted, 0, near[KERNEL_AT + 16 * at : KERNEL_AT + 16 * (at + 1)], last[0:1, TILE : TILE + 1])
    put_angles(level, cos_ref, sin_ref, ids, scale, last[:BEAMS, :TILE], last[BEAMS:, :TILE])


def reach_tables(level, near, ids, scale):
    angles = shape(2 * PART, TILE, dtype=F32)
    outs = [shape(1, 2 * TILE, 3 * TILE), angles, angles]
    return call(functools.partial(reach_kernel, level), outs, 3, 1 << 25, f"reach{level}")(near, ids, scale)


def merge(spread, main, reach, mix, write):
    rows = 2 * PART
    wide = len(reach) > 0
    odd = jnp.where(is_odd(), 1, 0)
    order = [(main, tile, tile + odd if wide else tile) for tile in range(TILES)]
    if wide:
        order.append((reach, 0, jnp.where(odd == 1, 0, TILES)))
    parts = []
    for (shifted, _, _), index, place in order:
        window = spread[:, pl.ds(aligned(place * TILE), 3 * TILE)]
        both = lax.dot_general(window, shifted[index], (((1,), (1,)), ((), ())), preferred_element_type=F32)
        real = both[:rows, :TILE] - both[rows:, TILE:]
        imag = both[:rows, TILE:] + both[rows:, :TILE]
        parts.append(jnp.concatenate([real, imag], axis=1).astype(BF))
    for ((_, cos_ref, sin_ref), index, place), part in zip(order, parts):
        lanes = slice(index * TILE, (index + 1) * TILE)
        mixed = jnp.dot(mix, part, preferred_element_type=F32)
        mixed_re = mixed[:, :TILE]
        mixed_im = mixed[:, TILE:]
        cosine = cos_ref[:, lanes]
        sine = sin_ref[:, lanes]
        out_re = (mixed_re * cosine + mixed_im * sine).astype(BF)
        out_im = (mixed_im * cosine - mixed_re * sine).astype(BF)
        write(pl.ds(aligned(place * TILE), TILE), out_re, out_im)


def level_kernel(level, *refs):
    wide = level in WIDE
    count = 3 if level == 0 else 6 if wide else 4
    data, rest = refs[:count], refs[count:]
    main, mix_ref, rest = rest[:3], rest[3], rest[4:]
    reach = ()
    if wide:
        reach, rest = rest[:3], rest[3:]
    *outs, spread = rest
    odd = is_odd()
    if wide:
        near = pl.ds(aligned(jnp.where(odd, 0, BLOCK + TILE)), REACH)
        far = pl.ds(aligned(jnp.where(odd, BLOCK + REACH, 0)), TILE)
        middle = pl.ds(aligned(jnp.where(odd, REACH, TILE)), BLOCK)
    else:
        far = pl.ds(aligned(jnp.where(odd, BLOCK + TILE, 0)), TILE)
        middle = pl.ds(aligned(jnp.where(odd, 0, TILE)), BLOCK + TILE)
    if level == 0:
        block, near_edge, far_edge = data
        for z in range(2):
            rows = pl.ds(2 * z * PART, 2 * PART)
            spread[rows, middle] = block[z].reshape(2 * PART, BLOCK)
            spread[rows, near] = near_edge[pl.ds(16 * z, 16)].reshape(2 * PART, REACH)
            spread[rows, far] = far_edge[z].reshape(2 * PART, TILE)
    else:
        for side in range(2):
            for z in range(2):
                rows = pl.ds((2 * z + side) * PART, PART)
                spread[rows, middle] = data[side][z]
                spread[rows, far] = data[((4, 3) if wide else (3, 2))[side]][z]
                if wide:
                    spread[rows, near] = data[(5, 2)[side]][z]
    held, sent = outs[:2]

    def write(lanes, out_re, out_im):
        for z, value in enumerate((out_re, out_im)):
            sent[z, :, lanes] = value[:PART]
            held[z, :, lanes] = value[PART:]

    merge(spread, main, reach, mix_ref[...], write)
    if level < LEVELS - 1:
        start = BLOCK if wide else BLOCK - TILE
        far = pl.ds(aligned(jnp.where(odd, start, 0)), TILE)
        near = pl.ds(aligned(jnp.where(odd, 0, BLOCK - REACH)), REACH)
        for side in range(2):
            outs[2 + side][...] = outs[side][:, :, far]
            if not wide:
                outs[4 + side][...] = outs[side][:, :, near]


def level_call(level, data, tables, reach):
    wide = level in WIDE
    outs = [shape(2, PART, BLOCK + TILE if wide else BLOCK)] * 2
    if level < LEVELS - 1:
        outs += [shape(2, PART, TILE)] * 2
        if not wide:
            outs += [shape(2, PART, REACH)] * 2
    operands = (*data, *tables, *reach)
    width = BLOCK + TILE + (REACH if wide else TILE)
    return call(
        functools.partial(level_kernel, level),
        outs,
        len(operands),
        TILES * 2 * (4 * PART * 384 * 256 + 4 * PART * PART * 256),
        f"merge{level}",
        [pltpu.VMEM((4 * PART, width), BF)],
    )(*operands)


def body(grad_image, range_kernel, band_offsets, beam_mix, ramp, baseline_ids, baseline_scale):
    pulses = lax.axis_size("pulse")
    ranges = lax.axis_size("range")
    near_pairs = [(i, i ^ 1) for i in range(ranges)]
    far_pairs = [(i, i + 1) for i in range(1, ranges - 1, 2)]
    far_pairs += [(t, s) for s, t in far_pairs]

    def move(value, mask, pairs):
        pairs = [(p * ranges + s, (p ^ mask) * ranges + t) for p in range(pulses) for s, t in pairs]
        return lax.ppermute(value, ("pulse", "range"), pairs)

    block = grad_image[0]
    ids = baseline_ids[None]
    scale = baseline_scale[None]
    near_pack, far_edge = take_edges(
        block,
        range_kernel.reshape(LEVELS, TILES, 16, 16, 2 * TILE),
        ramp.reshape(LEVELS, 2 * BEAMS, BLOCK),
        band_offsets,
    )
    near_pack = move(near_pack, 0, near_pairs)
    far_edge = move(far_edge, 0, far_pairs)
    state = (block, near_pack, far_edge)
    stay = [(i, i) for i in range(ranges)]
    tables = [make_tables(l, range_kernel, band_offsets, ramp, ids, scale, beam_mix) for l in range(LEVELS)]
    reach = [reach_tables(l, near_pack, ids, scale) if l in WIDE else () for l in range(LEVELS)]
    for level in range(LEVELS):
        if level == 1:
            state, tables, reach = lax.optimization_barrier((state, tables, reach))
        held, sent, *edges = level_call(level, state, tables[level], reach[level])
        mask = 2 ** BITS[level]
        got = move(sent, mask, stay)
        state = [held, got]
        if edges:
            far = edges[:2]
        if len(edges) > 2:
            state.append(move(edges[3], mask, near_pairs))
            state.append(move(far[1], mask, far_pairs))
            state.append(move(far[0], 0, far_pairs))
            state.append(move(edges[2], 0, near_pairs))
        elif edges:
            state.append(move(far[1], mask, far_pairs))
            state.append(move(far[0], 0, far_pairs))

    held = held.reshape(2, CHANNELS, BEAMS, BLOCK)
    got = got.reshape(2, CHANNELS, BEAMS, BLOCK)
    mine = bit_of(LEVELS - 1) == 1
    return jnp.concatenate([jnp.where(mine, got, held), jnp.where(mine, held, got)], axis=2)[None]


def solution(mesh):
    placed = (
        P("pulse", None, None, None, "range"),
        P(None, "range", None, None, None),
        P(None, "range"),
        P(None, "pulse", None, None, None),
        P(None, "pulse", None, None, "range"),
        P(),
        P(),
    )
    return jax.shard_map(
        body,
        mesh=mesh,
        in_specs=placed,
        out_specs=P("pulse", None, None, None, "range"),
        check_vma=False,
    )
```

```python
import functools
import jax
import jax.numpy as jnp
from jax import lax
from jax.experimental import pallas as pl
from jax.experimental.pallas import tpu as pltpu
from jax.sharding import PartitionSpec as P

TILE = 128
LEVELS = 4
CHANNELS = 16
BEAMS = 8
PART = CHANNELS * BEAMS
BITS = (4, 3, 2, 1)
BLOCK = 512
TILES = BLOCK // TILE
LAG = 2
VMEM_LIMIT = 24 * 1024 * 1024
BF = jnp.bfloat16
F32 = jnp.float32
VMEM = pl.BlockSpec(memory_space=pltpu.VMEM)
ANYWHERE = pl.BlockSpec(memory_space=pl.ANY)
WIDE = (0, 2)
REACH = 2 * TILE
KERNEL_AT = 32
RAMP_AT = KERNEL_AT + 16 * len(WIDE)
UNITS = RAMP_AT + len(WIDE)


def call(kernel, out_shape, count, flops, name, scratch=()):
    return pl.pallas_call(
        kernel,
        out_shape=out_shape,
        in_specs=[VMEM] * count,
        out_specs=[VMEM] * len(out_shape),
        scratch_shapes=list(scratch),
        compiler_params=pltpu.CompilerParams(vmem_limit_bytes=VMEM_LIMIT),
        cost_estimate=pl.CostEstimate(flops=flops, bytes_accessed=1 << 20, transcendentals=0),
        name=name,
    )


def shape(*dims, dtype=BF):
    return jax.ShapeDtypeStruct(dims, dtype)


def is_odd():
    return lax.axis_index("range") % 2 == 1


def bit_of(level):
    return lax.axis_index("pulse") // 2 ** BITS[level] % 2


def aligned(lane):
    return pl.multiple_of(lane, TILE)


def sincos(theta):
    turns = jnp.round(theta * 0.6366197723675814)
    rest = theta - turns * 1.5703125
    rest = rest - turns * 4.837512969970703e-4
    rest = rest - turns * 7.549789948768648e-8
    sq = rest * rest
    sine = rest + rest * sq * (-1.6666654611e-1 + sq * (8.3321608736e-3 - sq * 1.9515295891e-4))
    cosine = 1.0 - 0.5 * sq + sq * sq * (
        4.166664568298827e-2 + sq * (-1.388731625493765e-3 + sq * 2.443315711809948e-5)
    )
    quarter = turns.astype(jnp.int32)
    odd = (quarter & 1) == 1
    sin_sign = (quarter & 2) == 2
    cos_sign = ((quarter + 1) & 2) == 2
    out_sin = jnp.where(odd, cosine, sine)
    out_cos = jnp.where(odd, sine, cosine)
    return jnp.where(sin_sign, -out_sin, out_sin), jnp.where(cos_sign, -out_cos, out_cos)


def edges_kernel(image, taps, ramp, offsets, near, far, moves, sems):
    odd = is_odd()
    near_lanes = pl.ds(aligned(jnp.where(odd, 0, BLOCK - REACH)), REACH)
    far_lanes = pl.ds(aligned(jnp.where(odd, BLOCK - TILE, 0)), TILE)
    ramp_lanes = pl.ds(aligned(jnp.where(odd, 0, BLOCK - TILE)), TILE)
    copies = [(offsets, moves)]
    for z in range(2):
        copies.append((image.at[z, :, :, near_lanes], near.at[pl.ds(16 * z, 16)]))
        copies.append((image.at[z, :, :, far_lanes], far.at[z]))
    for at, level in enumerate(WIDE):
        copies.append((taps.at[level, jnp.where(odd, 0, TILES - 1)], near.at[pl.ds(KERNEL_AT + 16 * at, 16)]))
        copies.append((ramp.at[level, :, ramp_lanes], near.at[RAMP_AT + at, :, pl.ds(0, TILE)]))
    copies = [pltpu.make_async_copy(s, t, sems.at[i]) for i, (s, t) in enumerate(copies)]
    for copy in copies:
        copy.start()
    copies[0].wait()
    values = moves[...].astype(F32)
    for at, level in enumerate(WIDE):
        row = values[level : level + 1]
        value = jnp.where(odd, row[:, 0:1], row[:, TILES - 1 : TILES])
        near[RAMP_AT + at, :, TILE:] = jnp.broadcast_to(value, (16, REACH - TILE)).astype(BF)
    for copy in copies[1:]:
        copy.wait()


def take_edges(image, taps, ramp, offsets):
    return pl.pallas_call(
        edges_kernel,
        out_shape=[shape(UNITS, 16, REACH), shape(2, CHANNELS, 2 * BEAMS, TILE)],
        in_specs=[ANYWHERE] * 4,
        out_specs=[VMEM] * 2,
        scratch_shapes=[pltpu.VMEM((LEVELS, TILES), jnp.int32), pltpu.SemaphoreType.DMA((9,))],
        compiler_params=pltpu.CompilerParams(vmem_limit_bytes=56 * 1024 * 1024),
        cost_estimate=pl.CostEstimate(flops=1 << 20, bytes_accessed=1 << 20, transcendentals=0),
        name="edges",
    )(image, taps, ramp, offsets)


def put_shifted(shifted, tile, taps, offset):
    row = lax.broadcasted_iota(jnp.int32, (2 * TILE, 3 * TILE), 0)
    col = lax.broadcasted_iota(jnp.int32, (2 * TILE, 3 * TILE), 1)
    gap = (col - row).astype(F32) - TILE // 2
    pick = jnp.where(gap == offset, 1.0, 0.0).astype(BF)
    flat = taps.reshape(2 * TILE, 2 * TILE)
    shifted[tile] = jnp.dot(flat, pick, preferred_element_type=F32).astype(BF)


def put_angles(level, cos_ref, sin_ref, ids, scale, first, second):
    phase = jnp.zeros((1, CHANNELS), F32)
    for baseline in range(8):
        phase = phase + jnp.where(ids[...] == baseline, scale[:, baseline : baseline + 1], 0.0)
    bit = bit_of(level)
    sent = jnp.where(bit == 1, first, second)
    held = jnp.where(bit == 1, second, first)
    for channel in range(CHANNELS):
        length = phase[:, channel : channel + 1]
        for side, angle in enumerate((sent, held)):
            sine, cosine = sincos(angle * length)
            at = pl.ds(side * PART + channel * BEAMS, BEAMS)
            cos_ref[at, :] = cosine
            sin_ref[at, :] = sine


def tables_kernel(level, taps, offsets, ramp, ids, scale, beam, shifted, cos_ref, sin_ref, mix_ref):
    moves = offsets[...].astype(F32)
    for tile in range(TILES):
        put_shifted(shifted, tile, taps[0, tile], moves[level : level + 1, tile : tile + 1])
    angles = ramp[0, 0].astype(F32)
    put_angles(level, cos_ref, sin_ref, ids, scale, angles[0], angles[1])

    size = 2 * PART
    bit = bit_of(level)
    row = lax.broadcasted_iota(jnp.int32, (size, 16), 0)
    want = lax.broadcasted_iota(jnp.int32, (size, 16), 1)
    child = jnp.where(row // PART == 1, bit, 1 - bit)
    choose = jnp.where(want == child * BEAMS + row % BEAMS, 1.0, 0.0).astype(BF)
    beams = beam[0, 0].astype(F32).reshape(16, 16).astype(BF)
    rows = jnp.dot(choose, beams, preferred_element_type=F32).astype(BF)
    have = lax.broadcasted_iota(jnp.int32, (16, size), 0)
    col = lax.broadcasted_iota(jnp.int32, (16, size), 1)
    if level == 0:
        source = col % 16
    else:
        before = bit_of(level - 1)
        source = jnp.where(col // PART == 0, before, 1 - before) * BEAMS + col % BEAMS
    spread = jnp.where(have == source, 1.0, 0.0).astype(BF)
    full = jnp.dot(rows, spread, preferred_element_type=F32)
    at_row = lax.broadcasted_iota(jnp.int32, (size, size), 0) // BEAMS % CHANNELS
    at_col = lax.broadcasted_iota(jnp.int32, (size, size), 1)
    at_col = at_col // 16 if level == 0 else at_col // BEAMS % CHANNELS
    mix_ref[...] = jnp.where(at_row == at_col, full, 0.0).astype(BF)


def make_tables(level, taps, offsets, ramp, ids, scale, beam_mix):
    part = pl.BlockSpec((1, TILES, 2, TILE, 2 * TILE), lambda i: (level, 0, 0, 0, 0))
    angle = pl.BlockSpec((1, 1, 2, BEAMS, BLOCK), lambda i: (level, 0, 0, 0, 0))
    beam = pl.BlockSpec((1, 1, 2, BEAMS, 16), lambda i: (level, 0, 0, 0, 0))
    angles = shape(2 * PART, BLOCK, dtype=F32)
    return pl.pallas_call(
        functools.partial(tables_kernel, level),
        grid=(1,),
        out_shape=[shape(TILES, 2 * TILE, 3 * TILE), angles, angles, shape(2 * PART, 2 * PART)],
        in_specs=[part, VMEM, angle, VMEM, VMEM, beam],
        out_specs=[VMEM] * 4,
        compiler_params=pltpu.CompilerParams(vmem_limit_bytes=VMEM_LIMIT),
        cost_estimate=pl.CostEstimate(flops=1 << 27, bytes_accessed=1 << 21, transcendentals=0),
        name=f"tables{level}",
    )(taps, offsets, ramp, ids, scale, beam_mix)


def reach_kernel(level, near, ids, scale, shifted, cos_ref, sin_ref):
    at = WIDE.index(level)
    last = near[RAMP_AT + at].astype(F32)
    put_shifted(shifted, 0, near[KERNEL_AT + 16 * at : KERNEL_AT + 16 * (at + 1)], last[0:1, TILE : TILE + 1])
    put_angles(level, cos_ref, sin_ref, ids, scale, last[:BEAMS, :TILE], last[BEAMS:, :TILE])


def reach_tables(level, near, ids, scale):
    angles = shape(2 * PART, TILE, dtype=F32)
    outs = [shape(1, 2 * TILE, 3 * TILE), angles, angles]
    return call(functools.partial(reach_kernel, level), outs, 3, 1 << 25, f"reach{level}")(near, ids, scale)


def merge(spread, main, reach, mix, write):
    rows = 2 * PART
    wide = len(reach) > 0
    odd = jnp.where(is_odd(), 1, 0)
    order = [(main, tile, tile + odd if wide else tile) for tile in range(TILES)]
    if wide:
        order.append((reach, 0, jnp.where(odd == 1, 0, TILES)))
    parts = []

    def finish(step):
        (_, cos_ref, sin_ref), index, place = order[step]
        lanes = slice(index * TILE, (index + 1) * TILE)
        mixed = jnp.dot(mix, parts[step], preferred_element_type=F32)
        mixed_re = mixed[:, :TILE]
        mixed_im = mixed[:, TILE:]
        cosine = cos_ref[:, lanes]
        sine = sin_ref[:, lanes]
        out_re = (mixed_re * cosine + mixed_im * sine).astype(BF)
        out_im = (mixed_im * cosine - mixed_re * sine).astype(BF)
        write(pl.ds(aligned(place * TILE), TILE), out_re, out_im)

    for (shifted, _, _), index, place in order:
        window = spread[:, pl.ds(aligned(place * TILE), 3 * TILE)]
        both = lax.dot_general(window, shifted[index], (((1,), (1,)), ((), ())), preferred_element_type=F32)
        real = both[:rows, :TILE] - both[rows:, TILE:]
        imag = both[:rows, TILE:] + both[rows:, :TILE]
        parts.append(jnp.concatenate([real, imag], axis=1).astype(BF))
        if len(parts) > LAG:
            finish(len(parts) - 1 - LAG)
    for step in range(max(len(order) - LAG, 0), len(order)):
        finish(step)


def level_kernel(level, *refs):
    wide = level in WIDE
    count = 3 if level == 0 else 6 if wide else 4
    data, rest = refs[:count], refs[count:]
    main, mix_ref, rest = rest[:3], rest[3], rest[4:]
    reach = ()
    if wide:
        reach, rest = rest[:3], rest[3:]
    *outs, spread = rest
    odd = is_odd()
    if wide:
        near = pl.ds(aligned(jnp.where(odd, 0, BLOCK + TILE)), REACH)
        far = pl.ds(aligned(jnp.where(odd, BLOCK + REACH, 0)), TILE)
        middle = pl.ds(aligned(jnp.where(odd, REACH, TILE)), BLOCK)
    else:
        far = pl.ds(aligned(jnp.where(odd, BLOCK + TILE, 0)), TILE)
        middle = pl.ds(aligned(jnp.where(odd, 0, TILE)), BLOCK + TILE)
    if level == 0:
        block, near_edge, far_edge = data
        for z in range(2):
            rows = pl.ds(2 * z * PART, 2 * PART)
            spread[rows, middle] = block[z].reshape(2 * PART, BLOCK)
            spread[rows, near] = near_edge[pl.ds(16 * z, 16)].reshape(2 * PART, REACH)
            spread[rows, far] = far_edge[z].reshape(2 * PART, TILE)
    else:
        for side in range(2):
            for z in range(2):
                rows = pl.ds((2 * z + side) * PART, PART)
                spread[rows, middle] = data[side][z]
                spread[rows, far] = data[((4, 3) if wide else (3, 2))[side]][z]
                if wide:
                    spread[rows, near] = data[(5, 2)[side]][z]
    held, sent = outs[:2]

    def write(lanes, out_re, out_im):
        for z, value in enumerate((out_re, out_im)):
            sent[z, :, lanes] = value[:PART]
            held[z, :, lanes] = value[PART:]

    merge(spread, main, reach, mix_ref[...], write)
    if level < LEVELS - 1:
        start = BLOCK if wide else BLOCK - TILE
        far = pl.ds(aligned(jnp.where(odd, start, 0)), TILE)
        near = pl.ds(aligned(jnp.where(odd, 0, BLOCK - REACH)), REACH)
        for side in range(2):
            outs[2 + side][...] = outs[side][:, :, far]
            if not wide:
                outs[4 + side][...] = outs[side][:, :, near]


def level_call(level, data, tables, reach):
    wide = level in WIDE
    outs = [shape(2, PART, BLOCK + TILE if wide else BLOCK)] * 2
    if level < LEVELS - 1:
        outs += [shape(2, PART, TILE)] * 2
        if not wide:
            outs += [shape(2, PART, REACH)] * 2
    operands = (*data, *tables, *reach)
    width = BLOCK + TILE + (REACH if wide else TILE)
    return call(
        functools.partial(level_kernel, level),
        outs,
        len(operands),
        TILES * 2 * (4 * PART * 384 * 256 + 4 * PART * PART * 256),
        f"merge{level}",
        [pltpu.VMEM((4 * PART, width), BF)],
    )(*operands)


def body(grad_image, range_kernel, band_offsets, beam_mix, ramp, baseline_ids, baseline_scale):
    pulses = lax.axis_size("pulse")
    ranges = lax.axis_size("range")
    near_pairs = [(i, i ^ 1) for i in range(ranges)]
    far_pairs = [(i, i + 1) for i in range(1, ranges - 1, 2)]
    far_pairs += [(t, s) for s, t in far_pairs]

    def move(value, mask, pairs):
        pairs = [(p * ranges + s, (p ^ mask) * ranges + t) for p in range(pulses) for s, t in pairs]
        return lax.ppermute(value, ("pulse", "range"), pairs)

    block = grad_image[0]
    ids = baseline_ids[None]
    scale = baseline_scale[None]
    near_pack, far_edge = take_edges(
        block,
        range_kernel.reshape(LEVELS, TILES, 16, 16, 2 * TILE),
        ramp.reshape(LEVELS, 2 * BEAMS, BLOCK),
        band_offsets,
    )
    near_pack = move(near_pack, 0, near_pairs)
    far_edge = move(far_edge, 0, far_pairs)
    state = (block, near_pack, far_edge)
    stay = [(i, i) for i in range(ranges)]
    tables = [make_tables(l, range_kernel, band_offsets, ramp, ids, scale, beam_mix) for l in range(LEVELS)]
    reach = [reach_tables(l, near_pack, ids, scale) if l in WIDE else () for l in range(LEVELS)]
    for level in range(LEVELS):
        if level == 1:
            state, tables, reach = lax.optimization_barrier((state, tables, reach))
        held, sent, *edges = level_call(level, state, tables[level], reach[level])
        mask = 2 ** BITS[level]
        got = move(sent, mask, stay)
        state = [held, got]
        if edges:
            far = edges[:2]
        if len(edges) > 2:
            state.append(move(edges[3], mask, near_pairs))
            state.append(move(far[1], mask, far_pairs))
            state.append(move(far[0], 0, far_pairs))
            state.append(move(edges[2], 0, near_pairs))
        elif edges:
            state.append(move(far[1], mask, far_pairs))
            state.append(move(far[0], 0, far_pairs))

    held = held.reshape(2, CHANNELS, BEAMS, BLOCK)
    got = got.reshape(2, CHANNELS, BEAMS, BLOCK)
    mine = bit_of(LEVELS - 1) == 1
    return jnp.concatenate([jnp.where(mine, got, held), jnp.where(mine, held, got)], axis=2)[None]


def solution(mesh):
    placed = (
        P("pulse", None, None, None, "range"),
        P(None, "range", None, None, None),
        P(None, "range"),
        P(None, "pulse", None, None, None),
        P(None, "pulse", None, None, "range"),
        P(),
        P(),
    )
    return jax.shard_map(
        body,
        mesh=mesh,
        in_specs=placed,
        out_specs=P("pulse", None, None, None, "range"),
        check_vma=False,
    )
```
